32 devices in a mesh: grp: 2 (over x), beam: 16 (over z, y, core).
Axes of the slice: x: 2, y: 2, z: 4, core: 2. Of those that a mesh axis runs over, the one named last changes fastest.
Arguments:
- s_matrix: bfloat16 [2, 2048, 16, 4096], P(None, ('grp', 'beam')), parts along dimension 1, may hold values from -6 to 6
- beam_weight: float32 [2, 2048], P(None, ('grp', 'beam')), parts along dimension 1, may hold values from -0.25 to 0.25
- probe_shift: int32 [256, 2], P(('grp', 'beam')), parts along dimension 0, may hold values from 0 to 191
- probe_cutoff: int32 [256], P(('grp', 'beam')), parts along dimension 0, may hold values from 64 to 512
- target: bfloat16 [2, 256, 4096], P(None, ('grp', 'beam')), parts along dimension 1, may hold values from -3 to 3
- target_exp: int32 [256], P(('grp', 'beam')), parts along dimension 0, may hold values from -1 to 2
Outputs:
- s_grad: bfloat16 [2, 2048, 16, 4096], P(None, ('grp', 'beam')), parts along dimension 1
The draws below stay inside these ranges and needn't reach their ends.
There are 2 independent parts, one for each index of `grp`. The reference program is written for one: setup_inputs(seed, part) draws one part's arguments, and reference() takes and returns one part's arrays. A program takes and returns all parts, laid end to end along the dimension named above; each array names one. Nothing has to cross between parts.
All inputs are finite; a program needn't handle non-finite values.
Results may differ from the reference program's by a relative error of at most 0.006.
Values may be sent and summed in bfloat16 or wider, within the bound.
No kernel may reach another device: no remote copies, remote signals or barrier semaphores. Data moves between devices by JAX's collectives and lax.ppermute only.
A program may use at most 128 MiB of HBM per device.

```python
import math
import jax
import jax.numpy as jnp
from jax import lax

SIDE = 32
BEAMS = 1024
PIX = 4096
GRID = 192
TILE_SIDE = 4
TILES = 16
PROBES = 128


def set_ends(array, own_key, smallest, top_value):
    extent = array.shape
    spot = [jax.random.randint(jax.random.fold_in(own_key, axis), (), 0, extent[axis]) for axis in range(len(extent))]
    array = array.at[tuple(spot)].set(smallest)
    longest = extent.index(max(extent))
    spot[longest] = (spot[longest] + 1) % extent[longest]
    return array.at[tuple(spot)].set(top_value)


def levels(stream_key, dims, split, smallest, top_value):
    loudness, own = 1.0, jax.random.fold_in(stream_key, 6)
    for axis_at, blocks in split:
        heights = jnp.exp(jax.random.uniform(jax.random.fold_in(own, axis_at), (blocks,), jnp.float32, smallest / len(split), top_value / len(split)))
        loudness = loudness * jnp.repeat(heights, dims[axis_at] // blocks).reshape([-1 if axis == axis_at else 1 for axis in range(len(dims))])
    return loudness


def bell_draw(own_key, shape, spread, most, split=(), kind=jnp.bfloat16):
    array = jax.random.normal(own_key, shape, jnp.float32) * spread
    if len(split) > 0:
        array = levels(own_key, shape, split, -0.22, 0.18) * array
    return jnp.clip(array, min=-most, max=most).astype(kind)


def setup_inputs(seed: int = 0, part: int = 0) -> dict:
    streams_of = jax.random.split(jax.random.key(seed), 7)
    own_keys = jax.random.split(jax.random.fold_in(streams_of[6], part), 7)
    s_matrix = bell_draw(own_keys[0], (2, BEAMS, TILES, PIX), 1.0, 6.0, ((1, 16),))
    beam_weight = bell_draw(own_keys[1], (2, BEAMS), (BEAMS // 2) ** -0.5, 0.25, ((1, 16),), jnp.float32)
    probe_shift = set_ends(jax.random.randint(own_keys[2], (PROBES, 2), 0, GRID), jax.random.fold_in(own_keys[2], 1), 0, GRID - 1).astype(jnp.int32)
    probe_cutoff = set_ends(jax.random.randint(own_keys[3], (PROBES,), BEAMS // 16, BEAMS // 2 + 1), jax.random.fold_in(own_keys[3], 1), BEAMS // 16, (BEAMS // 2 + 1) - 1).astype(jnp.int32)
    target = bell_draw(own_keys[4], (2, PROBES, PIX), 0.5, 3.0, ((1, 16),))
    target_exp = set_ends(jax.random.randint(own_keys[5], (PROBES,), -1, 3), jax.random.fold_in(own_keys[5], 1), -1, 2).astype(jnp.int32)
    return dict(s_matrix=s_matrix, beam_weight=beam_weight, probe_shift=probe_shift, probe_cutoff=probe_cutoff, target=target, target_exp=target_exp)


TWO_PI = 2.0 * math.pi

def window_of(shift):
    step = GRID // TILE_SIDE
    return shift[:, 0] // step * TILE_SIDE + shift[:, 1] // step

def coefficients(beam_index, weight, shift, cutoff):
    half = SIDE // 2
    freq_x = beam_index % SIDE - half
    freq_y = beam_index // SIDE - half
    ramp = (freq_x[None, :] * shift[:, 0:1] + freq_y[None, :] * shift[:, 1:2]) % GRID
    phase = ramp.astype(jnp.float32) * (TWO_PI / GRID)
    inside = (freq_x * freq_x + freq_y * freq_y)[None, :] <= cutoff[:, None]
    cosine = jnp.cos(phase)
    sine = jnp.sin(phase)
    w_real = weight[0][None, :]
    w_imag = weight[1][None, :]
    c_real = jnp.where(inside, w_real * cosine + w_imag * sine, 0.0)
    c_imag = jnp.where(inside, w_imag * cosine - w_real * sine, 0.0)
    return (c_real.astype(jnp.bfloat16), c_imag.astype(jnp.bfloat16))

def reference(s_matrix, beam_weight, probe_shift, probe_cutoff, target, target_exp):
    group = 32
    count = BEAMS // group
    s_blocks = s_matrix.reshape(2, count, group, TILES, PIX).transpose(1, 0, 2, 3, 4)
    w_blocks = beam_weight.reshape(2, count, group).transpose(1, 0, 2)
    starts = jnp.arange(count, dtype=jnp.int32) * group
    windows = window_of(probe_shift)
    onehot = windows[:, None] == jnp.arange(TILES, dtype=jnp.int32)[None, :]

    def expand(start, weight):
        index = start + jnp.arange(group, dtype=jnp.int32)
        c_real, c_imag = coefficients(index, weight, probe_shift, probe_cutoff)
        zero = jnp.zeros((), jnp.bfloat16)
        e_real = jnp.where(onehot[:, None, :], c_real[:, :, None], zero).reshape(PROBES, group * TILES)
        e_imag = jnp.where(onehot[:, None, :], c_imag[:, :, None], zero).reshape(PROBES, group * TILES)
        return (e_real, e_imag)

    def add_wave(total, item):
        start, block, weight = item
        e_real, e_imag = expand(start, weight)
        s_re = block[0].reshape(group * TILES, PIX)
        s_im = block[1].reshape(group * TILES, PIX)
        w_re = jnp.dot(e_real, s_re, preferred_element_type=jnp.float32) - jnp.dot(e_imag, s_im, preferred_element_type=jnp.float32)
        w_im = jnp.dot(e_real, s_im, preferred_element_type=jnp.float32) + jnp.dot(e_imag, s_re, preferred_element_type=jnp.float32)
        return ((total[0] + w_re, total[1] + w_im), None)
    empty = jnp.zeros((PROBES, PIX), jnp.float32)
    (wave_re, wave_im), _ = lax.scan(add_wave, (empty, empty), (starts, s_blocks, w_blocks))
    scale = jnp.exp2(target_exp.astype(jnp.float32))[None, :, None]
    scaled = target.astype(jnp.float32) * scale
    residual = (jnp.stack([wave_re, wave_im]) - scaled).astype(jnp.bfloat16)

    def grad(item):
        start, weight = item
        e_real, e_imag = expand(start, weight)
        g_re = jnp.dot(e_real.T, residual[0], preferred_element_type=jnp.float32) + jnp.dot(e_imag.T, residual[1], preferred_element_type=jnp.float32)
        g_im = jnp.dot(e_real.T, residual[1], preferred_element_type=jnp.float32) - jnp.dot(e_imag.T, residual[0], preferred_element_type=jnp.float32)
        return jnp.stack([g_re, g_im]).reshape(2, group, TILES, PIX).astype(jnp.bfloat16)
    blocks = lax.map(grad, (starts, w_blocks))
    return blocks.transpose(1, 0, 2, 3, 4).reshape(2, BEAMS, TILES, PIX)
```

```python
import functools
import math

import jax
import jax.numpy as jnp
from jax import lax
from jax.experimental import pallas as pl
from jax.experimental.pallas import tpu as pltpu
from jax.sharding import PartitionSpec as P

SIDE = 32
GRID = 192
TILE_SIDE = 4
TWO_PI = 2.0 * math.pi
CHUNKS = 2
FWD_COLUMNS = 512
BWD_COLUMNS = 512


def orders(count):
    masks = [1 << bit for bit in range(1, count.bit_length() - 1)]
    other = masks[:]
    if len(other) > 1:
        other[0], other[1] = other[1], other[0]
    return masks, other


def swap(x, count, stage):
    if stage < 0:
        pairs = [(i, i ^ 1) for i in range(count)]
    else:
        by_core = orders(count)
        pairs = [(i, i ^ by_core[i % 2][stage]) for i in range(count)]
    return lax.ppermute(x, "beam", pairs)


def forward_kernel(at_ref, s_ref, keep_ref, send_ref, a_ref):
    @pl.when(pl.program_id(0) == 0)
    def _():
        a_ref[...] = at_ref[...].T

    half = keep_ref.shape[0]
    wave = jnp.dot(a_ref[...], s_ref[...], preferred_element_type=jnp.float32)
    keep_ref[...] = wave[:half]
    send_ref[...] = wave[half:].astype(jnp.bfloat16)


def forward(at, s_flat, chunk, width):
    depth, rows = at.shape
    half = rows // 2
    steps = width // FWD_COLUMNS
    first = chunk * steps
    return pl.pallas_call(
        forward_kernel,
        grid=(steps,),
        in_specs=[
            pl.BlockSpec((depth, rows), lambda j: (0, 0)),
            pl.BlockSpec((depth, FWD_COLUMNS), lambda j: (0, first + j)),
        ],
        out_specs=[
            pl.BlockSpec((half, FWD_COLUMNS), lambda j: (0, j)),
            pl.BlockSpec((half, FWD_COLUMNS), lambda j: (0, j)),
        ],
        out_shape=[
            jax.ShapeDtypeStruct((half, width), jnp.float32),
            jax.ShapeDtypeStruct((half, width), jnp.bfloat16),
        ],
        scratch_shapes=[pltpu.VMEM((rows, depth), jnp.bfloat16)],
        compiler_params=pltpu.CompilerParams(vmem_limit_bytes=32 << 20),
        cost_estimate=pl.CostEstimate(
            flops=2 * rows * depth * width, bytes_accessed=2 * depth * width, transcendentals=0
        ),
    )(at, s_flat)


def backward_kernel(at_ref, own_ref, other_ref, *refs):
    out_ref = refs[-1]
    res = jnp.concatenate([own_ref[...], other_ref[...]], axis=0)
    out_ref[...] = jnp.dot(at_ref[...], res, preferred_element_type=jnp.float32).astype(jnp.bfloat16)


def backward(at, own, other, so_far, chunk, pixels):
    depth, rows = at.shape
    half, width = own.shape
    steps = width // BWD_COLUMNS
    first = chunk * steps
    extra = [] if so_far is None else [so_far]
    return pl.pallas_call(
        backward_kernel,
        grid=(steps,),
        in_specs=[
            pl.BlockSpec((depth, rows), lambda j: (0, 0)),
            pl.BlockSpec((half, BWD_COLUMNS), lambda j: (0, j)),
            pl.BlockSpec((half, BWD_COLUMNS), lambda j: (0, j)),
        ]
        + [pl.BlockSpec(memory_space=pl.ANY) for _ in extra],
        out_specs=pl.BlockSpec((depth, BWD_COLUMNS), lambda j: (0, first + j)),
        out_shape=jax.ShapeDtypeStruct((depth, pixels), jnp.bfloat16),
        input_output_aliases={3: 0} if extra else {},
        compiler_params=pltpu.CompilerParams(vmem_limit_bytes=32 << 20),
        cost_estimate=pl.CostEstimate(
            flops=2 * rows * depth * width, bytes_accessed=2 * depth * width, transcendentals=0
        ),
    )(at, own, other, *extra)


def expanded(first_beam, weight, shift_x, shift_y, cutoff, imaginary, tile_count):
    local = weight.shape[1]
    half = SIDE // 2
    beam = first_beam + jnp.arange(local, dtype=jnp.int32)
    freq_x = (beam % SIDE - half)[:, None]
    freq_y = (beam // SIDE - half)[:, None]
    ramp = (freq_x * shift_x[None, :] + freq_y * shift_y[None, :]) % GRID
    phase = ramp.astype(jnp.float32) * (TWO_PI / GRID)
    inside = freq_x * freq_x + freq_y * freq_y <= cutoff[None, :]
    cosine = jnp.cos(phase)
    sine = jnp.sin(phase)
    w_real = weight[0][:, None]
    w_imag = weight[1][:, None]
    c_real = jnp.where(inside, w_real * cosine + w_imag * sine, 0.0).astype(jnp.bfloat16)
    c_imag = jnp.where(inside, w_imag * cosine - w_real * sine, 0.0).astype(jnp.bfloat16)
    by_real = jnp.where(imaginary, c_imag, c_real)
    by_imag = jnp.where(imaginary, c_real, -c_imag)
    step = GRID // TILE_SIDE
    window = shift_x // step * TILE_SIDE + shift_y // step
    onehot = window[None, :] == jnp.arange(tile_count, dtype=jnp.int32)[:, None]
    both = jnp.stack([by_real, by_imag])
    spread = jnp.where(onehot[None, None], both[:, :, None, :], jnp.zeros((), jnp.bfloat16))
    return spread.reshape(2 * local * tile_count, shift_x.shape[0])


def body(count, s_matrix, beam_weight, probe_shift, probe_cutoff, target, target_exp):
    _, local, tile_count, pixels = s_matrix.shape
    stages = count.bit_length() - 2
    own_probes = probe_cutoff.shape[0]
    block = 2 * own_probes
    params = jnp.concatenate([probe_shift.T, probe_cutoff[None]], axis=0)
    params = jnp.concatenate([params, params], axis=1)
    for stage in list(range(stages - 1, -1, -1)) + [-1]:
        params = jnp.concatenate([params, swap(params, count, stage)], axis=1)
    rows = params.shape[1]
    imaginary = (jnp.arange(rows, dtype=jnp.int32) // own_probes % 2 == 1)[None, :]
    at = expanded(
        lax.axis_index("beam") * local, beam_weight, params[0], params[1], params[2], imaginary, tile_count
    )
    s_flat = s_matrix.reshape(2 * local * tile_count, pixels)
    scale = jnp.exp2(target_exp.astype(jnp.float32))[None, :, None]
    width = pixels // CHUNKS
    states = [forward(at, s_flat, chunk, width) for chunk in range(CHUNKS)]
    for stage in range(-1, stages):
        for chunk in range(CHUNKS):
            keep, send = states[chunk]
            total = keep + swap(send, count, stage).astype(jnp.float32)
            half = total.shape[0] // 2
            states[chunk] = (total[:half], total[half:].astype(jnp.bfloat16)) if stage < stages - 1 else total
    held = []
    for chunk in range(CHUNKS):
        part = target[:, :, chunk * width : (chunk + 1) * width].astype(jnp.float32) * scale
        held.append((states[chunk] - part.reshape(block, width)).astype(jnp.bfloat16))
    for stage in range(stages - 1, -1, -1):
        for chunk in range(CHUNKS):
            held[chunk] = jnp.concatenate([held[chunk], swap(held[chunk], count, stage)], axis=0)
    grad = None
    for chunk in range(CHUNKS):
        grad = backward(at, held[chunk], swap(held[chunk], count, -1), grad, chunk, pixels)
    return grad.reshape(2, local, tile_count, pixels)


def solution(mesh):
    return jax.shard_map(
        functools.partial(body, mesh.shape["beam"]),
        mesh=mesh,
        in_specs=(
            P(None, ("grp", "beam"), None, None),
            P(None, ("grp", "beam")),
            P(("grp", "beam"), None),
            P(("grp", "beam")),
            P(None, ("grp", "beam"), None),
            P(("grp", "beam")),
        ),
        out_specs=P(None, ("grp", "beam"), None, None),
        check_vma=False,
    )
```

```python
import functools
import math

import jax
import jax.numpy as jnp
from jax import lax
from jax.experimental import pallas as pl
from jax.experimental.pallas import tpu as pltpu
from jax.sharding import PartitionSpec as P

SIDE = 32
GRID = 192
TILE_SIDE = 4
TWO_PI = 2.0 * math.pi
CHUNKS = 2
PIECES = 2
FWD_COLUMNS = 512
BWD_ROWS = 256


def orders(count):
    masks = [1 << bit for bit in range(1, count.bit_length() - 1)]
    other = masks[:]
    if len(other) > 1:
        other[0], other[1] = other[1], other[0]
    return masks, other


def swap(x, count, stage):
    if stage < 0:
        pairs = [(i, i ^ 1) for i in range(count)]
    else:
        by_core = orders(count)
        pairs = [(i, i ^ by_core[i % 2][stage]) for i in range(count)]
    return lax.ppermute(x, "beam", pairs)


def stage_kernel(first_row, s_ref, out_ref, sem):
    rows, columns = out_ref.shape
    copy = pltpu.make_async_copy(s_ref.at[first_row : first_row + rows, 0:columns], out_ref, sem)
    copy.start()
    copy.wait()


def staged(s_flat, first_row, rows, columns):
    return pl.pallas_call(
        functools.partial(stage_kernel, first_row),
        in_specs=[pl.BlockSpec(memory_space=pl.ANY)],
        out_specs=pl.BlockSpec(memory_space=pltpu.VMEM),
        out_shape=pltpu.VMEM((rows, columns), s_flat.dtype),
        scratch_shapes=[pltpu.SemaphoreType.DMA],
        compiler_params=pltpu.CompilerParams(vmem_limit_bytes=20 << 20),
        cost_estimate=pl.CostEstimate(flops=0, bytes_accessed=2 * rows * columns, transcendentals=0),
    )(pltpu.with_memory_space_constraint(s_flat, pltpu.HBM))


def forward_kernel(count, next_column, waits, at_ref, *refs):
    pieces, refs = refs[:count], refs[count + waits :]
    copy = None
    if next_column is None:
        keep_ref, send_ref = refs
    else:
        s_ref, keep_ref, send_ref, next_ref, sem = refs
        columns = next_ref.shape[1]
        copy = pltpu.make_async_copy(s_ref.at[:, next_column : next_column + columns], next_ref, sem)
        copy.start()
    a = at_ref[...].T
    half, width = keep_ref.shape
    for start in range(0, width, FWD_COLUMNS):
        stop = start + FWD_COLUMNS
        wave, done = 0.0, 0
        for piece in pieces:
            rows = piece.shape[0]
            wave += jnp.dot(
                a[:, done : done + rows], piece[:, start:stop], preferred_element_type=jnp.float32
            )
            done += rows
        keep_ref[:, start:stop] = wave[:half]
        send_ref[:, start:stop] = wave[half:].astype(jnp.bfloat16)
    if copy is not None:
        copy.wait()


def forward(at, pieces, s_flat, next_column, after):
    depth, rows = at.shape
    half, width = rows // 2, pieces[0].shape[1]
    whole = pl.BlockSpec(memory_space=pltpu.VMEM)
    more = next_column is not None
    return pl.pallas_call(
        functools.partial(forward_kernel, len(pieces), next_column, len(after)),
        in_specs=[whole] * (1 + len(pieces)) + [pl.BlockSpec(memory_space=pl.ANY)] * (len(after) + more),
        out_specs=[whole] * (2 + more),
        out_shape=[
            jax.ShapeDtypeStruct((half, width), jnp.float32),
            jax.ShapeDtypeStruct((half, width), jnp.bfloat16),
        ]
        + [pltpu.VMEM((depth, width), s_flat.dtype)] * more,
        scratch_shapes=[pltpu.SemaphoreType.DMA] * more,
        compiler_params=pltpu.CompilerParams(vmem_limit_bytes=30 << 20),
        cost_estimate=pl.CostEstimate(
            flops=2 * rows * depth * width, bytes_accessed=2 * depth * width, transcendentals=0
        ),
    )(at, *pieces, *after, *([pltpu.with_memory_space_constraint(s_flat, pltpu.HBM)] if more else []))


def backward_kernel(first, at_ref, own_ref, other_ref, *refs):
    out_ref, held_ref, sems = refs[-3:]
    depth, width = held_ref.shape
    res = jnp.concatenate([own_ref[...], other_ref[...]], axis=0)
    copies = []
    for index, start in enumerate(range(0, depth, BWD_ROWS)):
        stop = start + BWD_ROWS
        held_ref[start:stop] = jnp.dot(
            at_ref[start:stop], res, preferred_element_type=jnp.float32
        ).astype(jnp.bfloat16)
        copies.append(
            pltpu.make_async_copy(
                held_ref.at[start:stop], out_ref.at[start:stop, first : first + width], sems.at[index]
            )
        )
        copies[-1].start()
    for copy in copies:
        copy.wait()


def backward(at, own, other, so_far, chunk, pixels):
    depth, rows = at.shape
    half, width = own.shape
    whole = pl.BlockSpec(memory_space=pltpu.VMEM)
    extra = [] if so_far is None else [so_far]
    return pl.pallas_call(
        functools.partial(backward_kernel, chunk * width),
        in_specs=[whole] * 3 + [pl.BlockSpec(memory_space=pl.ANY) for _ in extra],
        out_specs=pl.BlockSpec(memory_space=pl.ANY),
        out_shape=jax.ShapeDtypeStruct((depth, pixels), jnp.bfloat16),
        scratch_shapes=[
            pltpu.VMEM((depth, width), jnp.bfloat16),
            pltpu.SemaphoreType.DMA((depth // BWD_ROWS,)),
        ],
        input_output_aliases={3: 0} if extra else {},
        compiler_params=pltpu.CompilerParams(vmem_limit_bytes=30 << 20),
        cost_estimate=pl.CostEstimate(
            flops=2 * rows * depth * width, bytes_accessed=2 * depth * width, transcendentals=0
        ),
    )(at, own, other, *extra)


def joined(parts):
    total, done = 0, 0
    width = sum(part.shape[1] for part in parts)
    for part in parts:
        after = width - done - part.shape[1]
        total = total + lax.pad(part, jnp.zeros((), part.dtype), ((0, 0, 0), (done, after, 0)))
        done += part.shape[1]
    return total


def gathered(x, count):
    by_core = orders(count)

    def spread(core, block):
        return sum(mask for bit, mask in enumerate(reversed(by_core[core])) if block >> bit & 1)

    def fetch(x, source_of):
        return lax.ppermute(x, "beam", [(source_of(i), i) for i in range(count)])

    inner = count // 4
    x = joined([x] + [fetch(x, lambda i, k=k: i ^ spread(i % 2, k)) for k in range(1, inner)])
    return joined(
        [
            x,
            fetch(x, lambda i: i ^ spread(i % 2, inner)),
            fetch(x, lambda i: i ^ 1),
            fetch(x, lambda i: i ^ 1 ^ spread(1 - i % 2, inner)),
        ]
    )


def step(kernel, inputs, outputs, after):
    whole = pl.BlockSpec(memory_space=pltpu.VMEM)

    def run(*refs):
        kernel(*refs[: len(inputs)], *refs[len(inputs) + len(after) :])

    return pl.pallas_call(
        run,
        in_specs=[whole] * len(inputs) + [pl.BlockSpec(memory_space=pl.ANY)] * len(after),
        out_specs=[whole] * len(outputs),
        out_shape=[jax.ShapeDtypeStruct(shape, dtype) for shape, dtype in outputs],
        compiler_params=pltpu.CompilerParams(vmem_limit_bytes=4 << 20),
        cost_estimate=pl.CostEstimate(flops=0, bytes_accessed=0, transcendentals=0),
    )(*inputs, *after)


def halve_kernel(keep_ref, came_ref, near_ref, send_ref):
    half = near_ref.shape[0]
    near_ref[...] = keep_ref[:half] + came_ref[:half].astype(jnp.float32)
    send_ref[...] = (keep_ref[half:] + came_ref[half:].astype(jnp.float32)).astype(jnp.bfloat16)


def halved(keep, came, after):
    half = (keep.shape[0] // 2, keep.shape[1])
    return step(halve_kernel, [keep, came], [(half, jnp.float32), (half, jnp.bfloat16)], after)


def lessen_kernel(keep_ref, came_ref, target_ref, sum_ref, send_ref):
    block = target_ref.shape[0]
    total = keep_ref[...] + came_ref[...].astype(jnp.float32)
    own = total[:block] - target_ref[...].astype(jnp.float32)
    sum_ref[:block] = own
    sum_ref[block:] = total[block:]
    send_ref[:block] = own.astype(jnp.bfloat16)
    send_ref[block:] = total[block:].astype(jnp.bfloat16)


def lessened(keep, came, target, after):
    both = [(keep.shape, jnp.float32), (keep.shape, jnp.bfloat16)]
    return step(lessen_kernel, [keep, came, target], both, after)


def close_kernel(keep_ref, came_ref, out_ref):
    block = keep_ref.shape[0] // 2
    near, far = came_ref[block:], came_ref[:block]
    out_ref[:block] = (keep_ref[:block] + near.astype(jnp.float32)).astype(jnp.bfloat16)
    out_ref[block:] = (keep_ref[block:] + far.astype(jnp.float32)).astype(jnp.bfloat16)


def closed(keep, came, after):
    return step(close_kernel, [keep, came], [(keep.shape, jnp.bfloat16)], after)[0]


def stack_kernel(own_ref, came_ref, out_ref):
    rows = own_ref.shape[0]
    out_ref[:rows] = own_ref[...]
    out_ref[rows:] = came_ref[...]


def stacked(own, came, after):
    shape = (2 * own.shape[0], own.shape[1])
    return step(stack_kernel, [own, came], [(shape, own.dtype)], after)[0]


def expanded(first_beam, weight, shift_x, shift_y, cutoff, imaginary, tile_count):
    local = weight.shape[1]
    half = SIDE // 2
    beam = first_beam + jnp.arange(local, dtype=jnp.int32)
    freq_x = (beam % SIDE - half)[:, None]
    freq_y = (beam // SIDE - half)[:, None]
    ramp = (freq_x * shift_x[None, :] + freq_y * shift_y[None, :]) % GRID
    phase = ramp.astype(jnp.float32) * (TWO_PI / GRID)
    inside = freq_x * freq_x + freq_y * freq_y <= cutoff[None, :]
    cosine = jnp.cos(phase)
    sine = jnp.sin(phase)
    w_real = weight[0][:, None]
    w_imag = weight[1][:, None]
    c_real = jnp.where(inside, w_real * cosine + w_imag * sine, 0.0).astype(jnp.bfloat16)
    c_imag = jnp.where(inside, w_imag * cosine - w_real * sine, 0.0).astype(jnp.bfloat16)
    by_real = jnp.where(imaginary, c_imag, c_real)
    by_imag = jnp.where(imaginary, c_real, -c_imag)
    step = GRID // TILE_SIDE
    window = shift_x // step * TILE_SIDE + shift_y // step
    onehot = window[None, :] == jnp.arange(tile_count, dtype=jnp.int32)[:, None]
    both = jnp.stack([by_real, by_imag])
    spread = jnp.where(onehot[None, None], both[:, :, None, :], jnp.zeros((), jnp.bfloat16))
    return spread.reshape(2 * local * tile_count, shift_x.shape[0])


def body(count, s_matrix, beam_weight, probe_shift, probe_cutoff, target, target_exp):
    _, local, tile_count, pixels = s_matrix.shape
    stages = count.bit_length() - 2
    own_probes = probe_cutoff.shape[0]
    block = 2 * own_probes
    params = jnp.concatenate([probe_shift.T, probe_cutoff[None]], axis=0)
    params = jnp.concatenate([params, params], axis=1)
    params = gathered(params, count)
    rows = params.shape[1]
    imaginary = (jnp.arange(rows, dtype=jnp.int32) // own_probes % 2 == 1)[None, :]
    at = expanded(
        lax.axis_index("beam") * local, beam_weight, params[0], params[1], params[2], imaginary, tile_count
    )
    s_flat = s_matrix.reshape(2 * local * tile_count, pixels)
    scale = jnp.exp2(target_exp.astype(jnp.float32))[None, :, None]
    scaled = (target.astype(jnp.float32) * scale).astype(jnp.bfloat16).reshape(block, pixels)
    width = pixels // CHUNKS
    scaled = lax.optimization_barrier([scaled[:, c * width : (c + 1) * width] for c in range(CHUNKS)])
    depth = s_flat.shape[0] // PIECES
    pieces = [staged(s_flat, piece * depth, depth, width) for piece in range(PIECES)]
    states, after = [], []
    for chunk in range(CHUNKS):
        next_column = (chunk + 1) * width if chunk < CHUNKS - 1 else None
        keep, send, *pieces = forward(at, pieces, s_flat, next_column, after)
        states.append(halved(keep, swap(send, count, -1), after))
        after = [states[-1][1]]
    for stage in range(stages - 1):
        for chunk in range(CHUNKS):
            keep, send = states[chunk]
            after = [states[chunk + 1][1]] if stage == 0 and chunk < CHUNKS - 1 else []
            came = swap(send, count, stage)
            if stage < stages - 2:
                states[chunk] = halved(keep, came, after)
            else:
                states[chunk] = lessened(keep, came, scaled[chunk], after)
    held = [closed(keep, swap(send, count, stages - 1), []) for keep, send in states]
    for stage in range(stages - 2, -1, -1):
        held = [stacked(part, swap(part, count, stage), []) for part in held]
    grad = None
    for chunk in range(CHUNKS):
        grad = backward(at, held[chunk], swap(held[chunk], count, -1), grad, chunk, pixels)
    return grad.reshape(2, local, tile_count, pixels)


def solution(mesh):
    return jax.shard_map(
        functools.partial(body, mesh.shape["beam"]),
        mesh=mesh,
        in_specs=(
            P(None, ("grp", "beam"), None, None),
            P(None, ("grp", "beam")),
            P(("grp", "beam"), None),
            P(("grp", "beam")),
            P(None, ("grp", "beam"), None),
            P(("grp", "beam")),
        ),
        out_specs=P(None, ("grp", "beam"), None, None),
        check_vma=False,
    )
```

```python
import functools
import math

import jax
import jax.numpy as jnp
from jax import lax
from jax.experimental import pallas as pl
from jax.experimental.pallas import tpu as pltpu
from jax.sharding import PartitionSpec as P

SIDE = 32
GRID = 192
TILE_SIDE = 4
TWO_PI = 2.0 * math.pi
CHUNKS = 2
PIECES = 2
FWD_COLUMNS = 512
BWD_ROWS = 256


def orders(count):
    masks = [1 << bit for bit in range(1, count.bit_length() - 1)]
    other = masks[:]
    if len(other) > 1:
        other[0], other[1] = other[1], other[0]
    return masks, other


def swap(x, count, stage):
    if stage < 0:
        pairs = [(i, i ^ 1) for i in range(count)]
    else:
        by_core = orders(count)
        pairs = [(i, i ^ by_core[i % 2][stage]) for i in range(count)]
    return lax.ppermute(x, "beam", pairs)


def stage_kernel(first_row, s_ref, out_ref, sem):
    rows, columns = out_ref.shape
    copy = pltpu.make_async_copy(s_ref.at[first_row : first_row + rows, 0:columns], out_ref, sem)
    copy.start()
    copy.wait()


def staged(s_flat, first_row, rows, columns):
    return pl.pallas_call(
        functools.partial(stage_kernel, first_row),
        in_specs=[pl.BlockSpec(memory_space=pl.ANY)],
        out_specs=pl.BlockSpec(memory_space=pltpu.VMEM),
        out_shape=pltpu.VMEM((rows, columns), s_flat.dtype),
        scratch_shapes=[pltpu.SemaphoreType.DMA],
        compiler_params=pltpu.CompilerParams(vmem_limit_bytes=20 << 20),
        cost_estimate=pl.CostEstimate(flops=0, bytes_accessed=2 * rows * columns, transcendentals=0),
    )(pltpu.with_memory_space_constraint(s_flat, pltpu.HBM))


def forward_kernel(count, next_column, waits, at_ref, *refs):
    pieces, refs = refs[:count], refs[count + waits :]
    copy = None
    if next_column is None:
        keep_ref, send_ref = refs
    else:
        s_ref, keep_ref, send_ref, next_ref, sem = refs
        columns = next_ref.shape[1]
        copy = pltpu.make_async_copy(s_ref.at[:, next_column : next_column + columns], next_ref, sem)
        copy.start()
    a = at_ref[...].T
    half, width = keep_ref.shape
    for start in range(0, width, FWD_COLUMNS):
        stop = start + FWD_COLUMNS
        wave, done = 0.0, 0
        for piece in pieces:
            rows = piece.shape[0]
            wave += jnp.dot(
                a[:, done : done + rows], piece[:, start:stop], preferred_element_type=jnp.float32
            )
            done += rows
        keep_ref[:, start:stop] = wave[:half]
        send_ref[:, start:stop] = wave[half:].astype(jnp.bfloat16)
    if copy is not None:
        copy.wait()


def forward(at, pieces, s_flat, next_column, after):
    depth, rows = at.shape
    half, width = rows // 2, pieces[0].shape[1]
    whole = pl.BlockSpec(memory_space=pltpu.VMEM)
    more = next_column is not None
    return pl.pallas_call(
        functools.partial(forward_kernel, len(pieces), next_column, len(after)),
        in_specs=[whole] * (1 + len(pieces)) + [pl.BlockSpec(memory_space=pl.ANY)] * (len(after) + more),
        out_specs=[whole] * (2 + more),
        out_shape=[
            jax.ShapeDtypeStruct((half, width), jnp.float32),
            jax.ShapeDtypeStruct((half, width), jnp.bfloat16),
        ]
        + [pltpu.VMEM((depth, width), s_flat.dtype)] * more,
        scratch_shapes=[pltpu.SemaphoreType.DMA] * more,
        compiler_params=pltpu.CompilerParams(vmem_limit_bytes=30 << 20),
        cost_estimate=pl.CostEstimate(
            flops=2 * rows * depth * width, bytes_accessed=2 * depth * width, transcendentals=0
        ),
    )(at, *pieces, *after, *([pltpu.with_memory_space_constraint(s_flat, pltpu.HBM)] if more else []))


def backward_kernel(first, at_ref, own_ref, other_ref, *refs):
    out_ref, held_ref, sems = refs[-3:]
    depth, width = held_ref.shape
    res = jnp.concatenate([own_ref[...], other_ref[...]], axis=0)
    copies = []
    for index, start in enumerate(range(0, depth, BWD_ROWS)):
        stop = start + BWD_ROWS
        held_ref[start:stop] = jnp.dot(
            at_ref[start:stop], res, preferred_element_type=jnp.float32
        ).astype(jnp.bfloat16)
        copies.append(
            pltpu.make_async_copy(
                held_ref.at[start:stop], out_ref.at[start:stop, first : first + width], sems.at[index]
            )
        )
        copies[-1].start()
    for copy in copies:
        copy.wait()


def backward(at, own, other, so_far, chunk, pixels):
    depth, rows = at.shape
    half, width = own.shape
    whole = pl.BlockSpec(memory_space=pltpu.VMEM)
    extra = [] if so_far is None else [so_far]
    return pl.pallas_call(
        functools.partial(backward_kernel, chunk * width),
        in_specs=[whole] * 3 + [pl.BlockSpec(memory_space=pl.ANY) for _ in extra],
        out_specs=pl.BlockSpec(memory_space=pl.ANY),
        out_shape=jax.ShapeDtypeStruct((depth, pixels), jnp.bfloat16),
        scratch_shapes=[
            pltpu.VMEM((depth, width), jnp.bfloat16),
            pltpu.SemaphoreType.DMA((depth // BWD_ROWS,)),
        ],
        input_output_aliases={3: 0} if extra else {},
        compiler_params=pltpu.CompilerParams(vmem_limit_bytes=30 << 20),
        cost_estimate=pl.CostEstimate(flops=0, bytes_accessed=0, transcendentals=0),
    )(at, own, other, *extra)


def joined(parts):
    total, done = 0, 0
    width = sum(part.shape[1] for part in parts)
    for part in parts:
        after = width - done - part.shape[1]
        total = total + lax.pad(part, jnp.zeros((), part.dtype), ((0, 0, 0), (done, after, 0)))
        done += part.shape[1]
    return total


def gathered(x, count, after):
    by_core = orders(count)

    def spread(core, block):
        return sum(mask for bit, mask in enumerate(reversed(by_core[core])) if block >> bit & 1)

    def fetch(x, source_of):
        return lax.ppermute(x, "beam", [(source_of(i), i) for i in range(count)])

    inner = count // 4
    parts = [x] + [fetch(x, lambda i, k=k: i ^ spread(i % 2, k)) for k in range(1, inner)]
    x = beside(parts, after)
    return joined(
        [
            x,
            fetch(x, lambda i: i ^ spread(i % 2, inner)),
            fetch(x, lambda i: i ^ 1),
            fetch(x, lambda i: i ^ 1 ^ spread(1 - i % 2, inner)),
        ]
    )


def step(kernel, inputs, outputs, after):
    whole = pl.BlockSpec(memory_space=pltpu.VMEM)

    def run(*refs):
        kernel(*refs[: len(inputs)], *refs[len(inputs) + len(after) :])

    return pl.pallas_call(
        run,
        in_specs=[whole] * len(inputs) + [pl.BlockSpec(memory_space=pl.ANY)] * len(after),
        out_specs=[whole] * len(outputs),
        out_shape=[jax.ShapeDtypeStruct(shape, dtype) for shape, dtype in outputs],
        compiler_params=pltpu.CompilerParams(vmem_limit_bytes=4 << 20),
        cost_estimate=pl.CostEstimate(flops=0, bytes_accessed=0, transcendentals=0),
    )(*inputs, *after)


def beside_kernel(*refs):
    done = 0
    for part_ref in refs[:-1]:
        width = part_ref.shape[1]
        refs[-1][:, done : done + width] = part_ref[...]
        done += width


def beside(parts, after):
    shape = (parts[0].shape[0], sum(part.shape[1] for part in parts))
    return step(beside_kernel, parts, [(shape, parts[0].dtype)], after)[0]


def halve_kernel(keep_ref, came_ref, near_ref, send_ref):
    half = near_ref.shape[0]
    near_ref[...] = keep_ref[:half] + came_ref[:half].astype(jnp.float32)
    send_ref[...] = (keep_ref[half:] + came_ref[half:].astype(jnp.float32)).astype(jnp.bfloat16)


def halved(keep, came, after):
    half = (keep.shape[0] // 2, keep.shape[1])
    return step(halve_kernel, [keep, came], [(half, jnp.float32), (half, jnp.bfloat16)], after)


def lessen_kernel(keep_ref, came_ref, target_ref, sum_ref, send_ref):
    block = target_ref.shape[0]
    total = keep_ref[...] + came_ref[...].astype(jnp.float32)
    own = total[:block] - target_ref[...].astype(jnp.float32)
    sum_ref[:block] = own
    sum_ref[block:] = total[block:]
    send_ref[:block] = own.astype(jnp.bfloat16)
    send_ref[block:] = total[block:].astype(jnp.bfloat16)


def lessened(keep, came, target, after):
    both = [(keep.shape, jnp.float32), (keep.shape, jnp.bfloat16)]
    return step(lessen_kernel, [keep, came, target], both, after)


def close_kernel(keep_ref, came_ref, out_ref):
    block = keep_ref.shape[0] // 2
    near, far = came_ref[block:], came_ref[:block]
    out_ref[:block] = (keep_ref[:block] + near.astype(jnp.float32)).astype(jnp.bfloat16)
    out_ref[block:] = (keep_ref[block:] + far.astype(jnp.float32)).astype(jnp.bfloat16)


def closed(keep, came, after):
    return step(close_kernel, [keep, came], [(keep.shape, jnp.bfloat16)], after)[0]


def stack_kernel(own_ref, came_ref, out_ref):
    rows = own_ref.shape[0]
    out_ref[:rows] = own_ref[...]
    out_ref[rows:] = came_ref[...]


def stacked(own, came, after):
    shape = (2 * own.shape[0], own.shape[1])
    return step(stack_kernel, [own, came], [(shape, own.dtype)], after)[0]


def expanded(first_beam, weight, shift_x, shift_y, cutoff, imaginary, tile_count):
    local = weight.shape[1]
    half = SIDE // 2
    beam = first_beam + jnp.arange(local, dtype=jnp.int32)
    freq_x = (beam % SIDE - half)[:, None]
    freq_y = (beam // SIDE - half)[:, None]
    ramp = (freq_x * shift_x[None, :] + freq_y * shift_y[None, :]) % GRID
    phase = ramp.astype(jnp.float32) * (TWO_PI / GRID)
    inside = freq_x * freq_x + freq_y * freq_y <= cutoff[None, :]
    cosine = jnp.cos(phase)
    sine = jnp.sin(phase)
    w_real = weight[0][:, None]
    w_imag = weight[1][:, None]
    c_real = jnp.where(inside, w_real * cosine + w_imag * sine, 0.0).astype(jnp.bfloat16)
    c_imag = jnp.where(inside, w_imag * cosine - w_real * sine, 0.0).astype(jnp.bfloat16)
    by_real = jnp.where(imaginary, c_imag, c_real)
    by_imag = jnp.where(imaginary, c_real, -c_imag)
    step = GRID // TILE_SIDE
    window = shift_x // step * TILE_SIDE + shift_y // step
    onehot = window[None, :] == jnp.arange(tile_count, dtype=jnp.int32)[:, None]
    both = jnp.stack([by_real, by_imag])
    spread = jnp.where(onehot[None, None], both[:, :, None, :], jnp.zeros((), jnp.bfloat16))
    return spread.reshape(2 * local * tile_count, shift_x.shape[0])


def body(count, s_matrix, beam_weight, probe_shift, probe_cutoff, target, target_exp):
    _, local, tile_count, pixels = s_matrix.shape
    stages = count.bit_length() - 2
    own_probes = probe_cutoff.shape[0]
    block = 2 * own_probes
    params = jnp.concatenate([probe_shift.T, probe_cutoff[None]], axis=0)
    params = jnp.concatenate([params, params], axis=1)
    s_flat = s_matrix.reshape(2 * local * tile_count, pixels)
    depth = s_flat.shape[0] // PIECES
    width = pixels // CHUNKS
    pieces = [staged(s_flat, piece * depth, depth, width) for piece in range(PIECES)]
    params = gathered(params, count, pieces[:1])
    rows = params.shape[1]
    imaginary = (jnp.arange(rows, dtype=jnp.int32) // own_probes % 2 == 1)[None, :]
    at = expanded(
        lax.axis_index("beam") * local, beam_weight, params[0], params[1], params[2], imaginary, tile_count
    )
    scale = jnp.exp2(target_exp.astype(jnp.float32))[None, :, None]
    scaled = (target.astype(jnp.float32) * scale).astype(jnp.bfloat16).reshape(block, pixels)
    scaled = lax.optimization_barrier([scaled[:, c * width : (c + 1) * width] for c in range(CHUNKS)])
    states, after = [], []
    for chunk in range(CHUNKS):
        next_column = (chunk + 1) * width if chunk < CHUNKS - 1 else None
        keep, send, *pieces = forward(at, pieces, s_flat, next_column, after)
        states.append(halved(keep, swap(send, count, -1), after))
        after = [states[-1][1]]
    for stage in range(stages - 1):
        for chunk in range(CHUNKS):
            keep, send = states[chunk]
            after = [states[chunk + 1][1]] if stage == 0 and chunk < CHUNKS - 1 else []
            came = swap(send, count, stage)
            if stage < stages - 2:
                states[chunk] = halved(keep, came, after)
            else:
                states[chunk] = lessened(keep, came, scaled[chunk], after)
    held = [closed(keep, swap(send, count, stages - 1), []) for keep, send in states]
    for stage in range(stages - 2, -1, -1):
        held = [stacked(part, swap(part, count, stage), []) for part in held]
    grad = None
    for chunk in range(CHUNKS):
        grad = backward(at, held[chunk], swap(held[chunk], count, -1), grad, chunk, pixels)
    return grad.reshape(2, local, tile_count, pixels)


def solution(mesh):
    return jax.shard_map(
        functools.partial(body, mesh.shape["beam"]),
        mesh=mesh,
        in_specs=(
            P(None, ("grp", "beam"), None, None),
            P(None, ("grp", "beam")),
            P(("grp", "beam"), None),
            P(("grp", "beam")),
            P(None, ("grp", "beam"), None),
            P(("grp", "beam")),
        ),
        out_specs=P(None, ("grp", "beam"), None, None),
        check_vma=False,
    )
```

```python
import functools
import math

import jax
import jax.numpy as jnp
from jax import lax
from jax.experimental import pallas as pl
from jax.experimental.pallas import tpu as pltpu
from jax.sharding import PartitionSpec as P

SIDE = 32
GRID = 192
TILE_SIDE = 4
TWO_PI = 2.0 * math.pi
CHUNKS = 2
PIECES = 2
FWD_COLUMNS = 512
BWD_ROWS = 256


def orders(count):
    masks = [1 << bit for bit in range(1, count.bit_length() - 1)]
    other = masks[:]
    if len(other) > 1:
        other[0], other[1] = other[1], other[0]
    return masks, other


def swap(x, count, stage):
    if stage < 0:
        pairs = [(i, i ^ 1) for i in range(count)]
    else:
        by_core = orders(count)
        pairs = [(i, i ^ by_core[i % 2][stage]) for i in range(count)]
    return lax.ppermute(x, "beam", pairs)


def stage_kernel(first_row, s_ref, out_ref, sem):
    rows, columns = out_ref.shape
    copy = pltpu.make_async_copy(s_ref.at[first_row : first_row + rows, 0:columns], out_ref, sem)
    copy.start()
    copy.wait()


def staged(s_flat, first_row, rows, columns):
    return pl.pallas_call(
        functools.partial(stage_kernel, first_row),
        in_specs=[pl.BlockSpec(memory_space=pl.ANY)],
        out_specs=pl.BlockSpec(memory_space=pltpu.VMEM),
        out_shape=pltpu.VMEM((rows, columns), s_flat.dtype),
        scratch_shapes=[pltpu.SemaphoreType.DMA],
        compiler_params=pltpu.CompilerParams(vmem_limit_bytes=20 << 20),
        cost_estimate=pl.CostEstimate(flops=0, bytes_accessed=2 * rows * columns, transcendentals=0),
    )(pltpu.with_memory_space_constraint(s_flat, pltpu.HBM))


def forward_kernel(count, waits, first, fetch, at_ref, *refs):
    pieces, refs = refs[:count], refs[count + waits :]
    copy = None
    if fetch is None:
        (out_ref,) = refs
    else:
        s_ref, out_ref, next_ref, sem = refs
        copy = pltpu.make_async_copy(s_ref.at[fetch], next_ref, sem)
        copy.start()
    rows, width = out_ref.shape
    a = at_ref[:, first : first + rows].T
    for start in range(0, width, FWD_COLUMNS):
        stop = start + FWD_COLUMNS
        wave, done = 0.0, 0
        for piece in pieces:
            depth = piece.shape[0]
            wave += jnp.dot(
                a[:, done : done + depth], piece[:, start:stop], preferred_element_type=jnp.float32
            )
            done += depth
        out_ref[:, start:stop] = wave.astype(out_ref.dtype)
    if copy is not None:
        copy.wait()


def forward(at, pieces, first, dtype, s_flat, fetch, after):
    depth, rows = at.shape[0], at.shape[1] // 2
    width = pieces[0].shape[1]
    whole = pl.BlockSpec(memory_space=pltpu.VMEM)
    more = fetch is not None
    block = [pltpu.VMEM(tuple(part.stop - part.start for part in fetch), s_flat.dtype)] if more else []
    return pl.pallas_call(
        functools.partial(forward_kernel, len(pieces), len(after), first, fetch),
        in_specs=[whole] * (1 + len(pieces)) + [pl.BlockSpec(memory_space=pl.ANY)] * (len(after) + more),
        out_specs=[whole] * (1 + more),
        out_shape=[jax.ShapeDtypeStruct((rows, width), dtype)] + block,
        scratch_shapes=[pltpu.SemaphoreType.DMA] * more,
        compiler_params=pltpu.CompilerParams(vmem_limit_bytes=30 << 20),
        cost_estimate=pl.CostEstimate(
            flops=2 * rows * depth * width, bytes_accessed=2 * depth * width, transcendentals=0
        ),
    )(at, *pieces, *after, *([pltpu.with_memory_space_constraint(s_flat, pltpu.HBM)] if more else []))


def backward_kernel(first, at_ref, own_ref, other_ref, *refs):
    out_ref, held_ref, sems = refs[-3:]
    depth, width = held_ref.shape
    res = jnp.concatenate([own_ref[...], other_ref[...]], axis=0)
    copies = []
    for index, start in enumerate(range(0, depth, BWD_ROWS)):
        stop = start + BWD_ROWS
        held_ref[start:stop] = jnp.dot(
            at_ref[start:stop], res, preferred_element_type=jnp.float32
        ).astype(jnp.bfloat16)
        copies.append(
            pltpu.make_async_copy(
                held_ref.at[start:stop], out_ref.at[start:stop, first : first + width], sems.at[index]
            )
        )
        copies[-1].start()
    for copy in copies:
        copy.wait()


def backward(at, own, other, so_far, chunk, pixels):
    depth, rows = at.shape
    half, width = own.shape
    whole = pl.BlockSpec(memory_space=pltpu.VMEM)
    extra = [] if so_far is None else [so_far]
    return pl.pallas_call(
        functools.partial(backward_kernel, chunk * width),
        in_specs=[whole] * 3 + [pl.BlockSpec(memory_space=pl.ANY) for _ in extra],
        out_specs=pl.BlockSpec(memory_space=pl.ANY),
        out_shape=jax.ShapeDtypeStruct((depth, pixels), jnp.bfloat16),
        scratch_shapes=[
            pltpu.VMEM((depth, width), jnp.bfloat16),
            pltpu.SemaphoreType.DMA((depth // BWD_ROWS,)),
        ],
        input_output_aliases={3: 0} if extra else {},
        compiler_params=pltpu.CompilerParams(vmem_limit_bytes=30 << 20),
        cost_estimate=pl.CostEstimate(flops=0, bytes_accessed=0, transcendentals=0),
    )(at, own, other, *extra)


def joined(parts):
    total, done = 0, 0
    width = sum(part.shape[1] for part in parts)
    for part in parts:
        after = width - done - part.shape[1]
        total = total + lax.pad(part, jnp.zeros((), part.dtype), ((0, 0, 0), (done, after, 0)))
        done += part.shape[1]
    return total


def gathered(x, count, after):
    by_core = orders(count)

    def spread(core, block):
        return sum(mask for bit, mask in enumerate(reversed(by_core[core])) if block >> bit & 1)

    def fetch(x, source_of):
        return lax.ppermute(x, "beam", [(source_of(i), i) for i in range(count)])

    inner = count // 4
    parts = [x] + [fetch(x, lambda i, k=k: i ^ spread(i % 2, k)) for k in range(1, inner)]
    x = beside(parts, after)
    return joined(
        [
            x,
            fetch(x, lambda i: i ^ spread(i % 2, inner)),
            fetch(x, lambda i: i ^ 1),
            fetch(x, lambda i: i ^ 1 ^ spread(1 - i % 2, inner)),
        ]
    )


def step(kernel, inputs, outputs, after):
    whole = pl.BlockSpec(memory_space=pltpu.VMEM)

    def run(*refs):
        kernel(*refs[: len(inputs)], *refs[len(inputs) + len(after) :])

    return pl.pallas_call(
        run,
        in_specs=[whole] * len(inputs) + [pl.BlockSpec(memory_space=pl.ANY)] * len(after),
        out_specs=[whole] * len(outputs),
        out_shape=[jax.ShapeDtypeStruct(shape, dtype) for shape, dtype in outputs],
        compiler_params=pltpu.CompilerParams(vmem_limit_bytes=4 << 20),
        cost_estimate=pl.CostEstimate(flops=0, bytes_accessed=0, transcendentals=0),
    )(*inputs, *after)


def beside_kernel(*refs):
    done = 0
    for part_ref in refs[:-1]:
        width = part_ref.shape[1]
        refs[-1][:, done : done + width] = part_ref[...]
        done += width


def beside(parts, after):
    shape = (parts[0].shape[0], sum(part.shape[1] for part in parts))
    return step(beside_kernel, parts, [(shape, parts[0].dtype)], after)[0]


def halve_kernel(keep_ref, came_ref, near_ref, send_ref):
    half = near_ref.shape[0]
    near_ref[...] = keep_ref[:half] + came_ref[:half].astype(jnp.float32)
    send_ref[...] = (keep_ref[half:] + came_ref[half:].astype(jnp.float32)).astype(jnp.bfloat16)


def halved(keep, came, after):
    half = (keep.shape[0] // 2, keep.shape[1])
    return step(halve_kernel, [keep, came], [(half, jnp.float32), (half, jnp.bfloat16)], after)


def lessen_kernel(keep_ref, came_ref, target_ref, sum_ref, send_ref):
    block = target_ref.shape[0]
    total = keep_ref[...] + came_ref[...].astype(jnp.float32)
    own = total[:block] - target_ref[...].astype(jnp.float32)
    sum_ref[:block] = own
    sum_ref[block:] = total[block:]
    send_ref[:block] = own.astype(jnp.bfloat16)
    send_ref[block:] = total[block:].astype(jnp.bfloat16)


def lessened(keep, came, target, after):
    both = [(keep.shape, jnp.float32), (keep.shape, jnp.bfloat16)]
    return step(lessen_kernel, [keep, came, target], both, after)


def close_kernel(keep_ref, came_ref, out_ref):
    block = keep_ref.shape[0] // 2
    near, far = came_ref[block:], came_ref[:block]
    out_ref[:block] = (keep_ref[:block] + near.astype(jnp.float32)).astype(jnp.bfloat16)
    out_ref[block:] = (keep_ref[block:] + far.astype(jnp.float32)).astype(jnp.bfloat16)


def closed(keep, came, after):
    return step(close_kernel, [keep, came], [(keep.shape, jnp.bfloat16)], after)[0]


def stack_kernel(own_ref, came_ref, out_ref):
    rows = own_ref.shape[0]
    out_ref[:rows] = own_ref[...]
    out_ref[rows:] = came_ref[...]


def stacked(own, came, after):
    shape = (2 * own.shape[0], own.shape[1])
    return step(stack_kernel, [own, came], [(shape, own.dtype)], after)[0]


def expanded(first_beam, weight, shift_x, shift_y, cutoff, imaginary, tile_count):
    local = weight.shape[1]
    half = SIDE // 2
    beam = first_beam + jnp.arange(local, dtype=jnp.int32)
    freq_x = (beam % SIDE - half)[:, None]
    freq_y = (beam // SIDE - half)[:, None]
    ramp = (freq_x * shift_x[None, :] + freq_y * shift_y[None, :]) % GRID
    phase = ramp.astype(jnp.float32) * (TWO_PI / GRID)
    inside = freq_x * freq_x + freq_y * freq_y <= cutoff[None, :]
    cosine = jnp.cos(phase)
    sine = jnp.sin(phase)
    w_real = weight[0][:, None]
    w_imag = weight[1][:, None]
    c_real = jnp.where(inside, w_real * cosine + w_imag * sine, 0.0).astype(jnp.bfloat16)
    c_imag = jnp.where(inside, w_imag * cosine - w_real * sine, 0.0).astype(jnp.bfloat16)
    by_real = jnp.where(imaginary, c_imag, c_real)
    by_imag = jnp.where(imaginary, c_real, -c_imag)
    step = GRID // TILE_SIDE
    window = shift_x // step * TILE_SIDE + shift_y // step
    onehot = window[None, :] == jnp.arange(tile_count, dtype=jnp.int32)[:, None]
    both = jnp.stack([by_real, by_imag])
    spread = jnp.where(onehot[None, None], both[:, :, None, :], jnp.zeros((), jnp.bfloat16))
    return spread.reshape(2 * local * tile_count, shift_x.shape[0])


def body(count, s_matrix, beam_weight, probe_shift, probe_cutoff, target, target_exp):
    _, local, tile_count, pixels = s_matrix.shape
    stages = count.bit_length() - 2
    own_probes = probe_cutoff.shape[0]
    block = 2 * own_probes
    params = jnp.concatenate([probe_shift.T, probe_cutoff[None]], axis=0)
    params = jnp.concatenate([params, params], axis=1)
    s_flat = s_matrix.reshape(2 * local * tile_count, pixels)
    depth = s_flat.shape[0] // PIECES
    width = pixels // CHUNKS
    pieces = [staged(s_flat, piece * depth, depth, width) for piece in range(PIECES)]
    params = gathered(params, count, pieces[:1])
    rows = params.shape[1]
    imaginary = (jnp.arange(rows, dtype=jnp.int32) // own_probes % 2 == 1)[None, :]
    at = expanded(
        lax.axis_index("beam") * local, beam_weight, params[0], params[1], params[2], imaginary, tile_count
    )
    scale = jnp.exp2(target_exp.astype(jnp.float32))[None, :, None]
    scaled = (target.astype(jnp.float32) * scale).astype(jnp.bfloat16).reshape(block, pixels)
    scaled = lax.optimization_barrier([scaled[:, c * width : (c + 1) * width] for c in range(CHUNKS)])
    states, after, total = [], [], s_flat.shape[0]
    for chunk in range(CHUNKS):
        columns = slice((chunk + 1) * width, (chunk + 2) * width)
        fetch = [(slice(row, row + total // 2), columns) for row in (0, total // 2)]
        fetch = fetch if chunk < CHUNKS - 1 else [None, None]
        send, *one = forward(at, pieces, rows // 2, jnp.bfloat16, s_flat, fetch[0], after)
        keep, *two = forward(at, pieces, 0, jnp.float32, s_flat, fetch[1], [send])
        pieces = one + two
        states.append(halved(keep, swap(send, count, -1), []))
        after = [states[-1][1]]
    for stage in range(stages - 1):
        for chunk in range(CHUNKS):
            keep, send = states[chunk]
            after = [states[chunk + 1][1]] if stage == 0 and chunk < CHUNKS - 1 else []
            came = swap(send, count, stage)
            if stage < stages - 2:
                states[chunk] = halved(keep, came, after)
            else:
                states[chunk] = lessened(keep, came, scaled[chunk], after)
    held = [closed(keep, swap(send, count, stages - 1), []) for keep, send in states]
    for stage in range(stages - 2, -1, -1):
        held = [stacked(part, swap(part, count, stage), []) for part in held]
    grad = None
    for chunk in range(CHUNKS):
        grad = backward(at, held[chunk], swap(held[chunk], count, -1), grad, chunk, pixels)
    return grad.reshape(2, local, tile_count, pixels)


def solution(mesh):
    return jax.shard_map(
        functools.partial(body, mesh.shape["beam"]),
        mesh=mesh,
        in_specs=(
            P(None, ("grp", "beam"), None, None),
            P(None, ("grp", "beam")),
            P(("grp", "beam"), None),
            P(("grp", "beam")),
            P(None, ("grp", "beam"), None),
            P(("grp", "beam")),
        ),
        out_specs=P(None, ("grp", "beam"), None, None),
        check_vma=False,
    )
```

```python
import functools
import math

import jax
import jax.numpy as jnp
from jax import lax
from jax.experimental import pallas as pl
from jax.experimental.pallas import tpu as pltpu
from jax.sharding import PartitionSpec as P

SIDE = 32
GRID = 192
TILE_SIDE = 4
TWO_PI = 2.0 * math.pi
CHUNKS = 2
PIECES = 2
FWD_COLUMNS = 512
BWD_ROWS = 128


def orders(count):
    masks = [1 << bit for bit in range(1, count.bit_length() - 1)]
    other = masks[:]
    if len(other) > 1:
        other[0], other[1] = other[1], other[0]
    return masks, other


def swap(x, count, stage):
    if stage < 0:
        pairs = [(i, i ^ 1) for i in range(count)]
    else:
        by_core = orders(count)
        pairs = [(i, i ^ by_core[i % 2][stage]) for i in range(count)]
    return lax.ppermute(x, "beam", pairs)


def stage_kernel(first_row, s_ref, out_ref, sem):
    rows, columns = out_ref.shape
    copy = pltpu.make_async_copy(s_ref.at[first_row : first_row + rows, 0:columns], out_ref, sem)
    copy.start()
    copy.wait()


def staged(s_flat, first_row, rows, columns):
    return pl.pallas_call(
        functools.partial(stage_kernel, first_row),
        in_specs=[pl.BlockSpec(memory_space=pl.ANY)],
        out_specs=pl.BlockSpec(memory_space=pltpu.VMEM),
        out_shape=pltpu.VMEM((rows, columns), s_flat.dtype),
        scratch_shapes=[pltpu.SemaphoreType.DMA],
        compiler_params=pltpu.CompilerParams(vmem_limit_bytes=20 << 20),
        cost_estimate=pl.CostEstimate(flops=0, bytes_accessed=2 * rows * columns, transcendentals=0),
    )(pltpu.with_memory_space_constraint(s_flat, pltpu.HBM))


def forward_kernel(count, waits, first, fetch, at_ref, *refs):
    pieces, refs = refs[:count], refs[count + waits :]
    copy = None
    if fetch is None:
        (out_ref,) = refs
    else:
        s_ref, out_ref, next_ref, sem = refs
        copy = pltpu.make_async_copy(s_ref.at[fetch], next_ref, sem)
        copy.start()
    rows, width = out_ref.shape
    a = at_ref[:, first : first + rows].T
    for start in range(0, width, FWD_COLUMNS):
        stop = start + FWD_COLUMNS
        wave, done = 0.0, 0
        for piece in pieces:
            depth = piece.shape[0]
            wave += jnp.dot(
                a[:, done : done + depth], piece[:, start:stop], preferred_element_type=jnp.float32
            )
            done += depth
        out_ref[:, start:stop] = wave.astype(out_ref.dtype)
    if copy is not None:
        copy.wait()


def forward(at, pieces, first, dtype, s_flat, fetch, after):
    depth, rows = at.shape[0], at.shape[1] // 2
    width = pieces[0].shape[1]
    whole = pl.BlockSpec(memory_space=pltpu.VMEM)
    more = fetch is not None
    block = [pltpu.VMEM(tuple(part.stop - part.start for part in fetch), s_flat.dtype)] if more else []
    return pl.pallas_call(
        functools.partial(forward_kernel, len(pieces), len(after), first, fetch),
        in_specs=[whole] * (1 + len(pieces)) + [pl.BlockSpec(memory_space=pl.ANY)] * (len(after) + more),
        out_specs=[whole] * (1 + more),
        out_shape=[jax.ShapeDtypeStruct((rows, width), dtype)] + block,
        scratch_shapes=[pltpu.SemaphoreType.DMA] * more,
        compiler_params=pltpu.CompilerParams(vmem_limit_bytes=30 << 20),
        cost_estimate=pl.CostEstimate(
            flops=2 * rows * depth * width, bytes_accessed=2 * depth * width, transcendentals=0
        ),
    )(at, *pieces, *after, *([pltpu.with_memory_space_constraint(s_flat, pltpu.HBM)] if more else []))


def backward_kernel(first, at_ref, own_ref, other_ref, *refs):
    out_ref, held_ref, sems = refs[-3:]
    depth, width = held_ref.shape
    res = jnp.concatenate([own_ref[...], other_ref[...]], axis=0)
    copies = []
    for index, start in enumerate(range(0, depth, BWD_ROWS)):
        stop = start + BWD_ROWS
        held_ref[start:stop] = jnp.dot(
            at_ref[start:stop], res, preferred_element_type=jnp.float32
        ).astype(jnp.bfloat16)
        copies.append(
            pltpu.make_async_copy(
                held_ref.at[start:stop], out_ref.at[start:stop, first : first + width], sems.at[index]
            )
        )
        copies[-1].start()
    for copy in copies:
        copy.wait()


def backward(at, own, other, so_far, chunk, pixels):
    depth, rows = at.shape
    half, width = own.shape
    whole = pl.BlockSpec(memory_space=pltpu.VMEM)
    extra = [] if so_far is None else [so_far]
    return pl.pallas_call(
        functools.partial(backward_kernel, chunk * width),
        in_specs=[whole] * 3 + [pl.BlockSpec(memory_space=pl.ANY) for _ in extra],
        out_specs=pl.BlockSpec(memory_space=pl.ANY),
        out_shape=jax.ShapeDtypeStruct((depth, pixels), jnp.bfloat16),
        scratch_shapes=[
            pltpu.VMEM((depth, width), jnp.bfloat16),
            pltpu.SemaphoreType.DMA((depth // BWD_ROWS,)),
        ],
        input_output_aliases={3: 0} if extra else {},
        compiler_params=pltpu.CompilerParams(vmem_limit_bytes=30 << 20),
        cost_estimate=pl.CostEstimate(flops=0, bytes_accessed=0, transcendentals=0),
    )(at, own, other, *extra)


def joined(parts):
    total, done = 0, 0
    width = sum(part.shape[1] for part in parts)
    for part in parts:
        after = width - done - part.shape[1]
        total = total + lax.pad(part, jnp.zeros((), part.dtype), ((0, 0, 0), (done, after, 0)))
        done += part.shape[1]
    return total


def gathered(x, count, after):
    by_core = orders(count)

    def spread(core, block):
        return sum(mask for bit, mask in enumerate(reversed(by_core[core])) if block >> bit & 1)

    def fetch(x, source_of):
        return lax.ppermute(x, "beam", [(source_of(i), i) for i in range(count)])

    inner = count // 4
    parts = [x] + [fetch(x, lambda i, k=k: i ^ spread(i % 2, k)) for k in range(1, inner)]
    x = beside(parts, after)
    return joined(
        [
            x,
            fetch(x, lambda i: i ^ spread(i % 2, inner)),
            fetch(x, lambda i: i ^ 1),
            fetch(x, lambda i: i ^ 1 ^ spread(1 - i % 2, inner)),
        ]
    )


def step(kernel, inputs, outputs, after):
    whole = pl.BlockSpec(memory_space=pltpu.VMEM)

    def run(*refs):
        kernel(*refs[: len(inputs)], *refs[len(inputs) + len(after) :])

    return pl.pallas_call(
        run,
        in_specs=[whole] * len(inputs) + [pl.BlockSpec(memory_space=pl.ANY)] * len(after),
        out_specs=[whole] * len(outputs),
        out_shape=[jax.ShapeDtypeStruct(shape, dtype) for shape, dtype in outputs],
        compiler_params=pltpu.CompilerParams(vmem_limit_bytes=4 << 20),
        cost_estimate=pl.CostEstimate(flops=0, bytes_accessed=0, transcendentals=0),
    )(*inputs, *after)


def beside_kernel(*refs):
    done = 0
    for part_ref in refs[:-1]:
        width = part_ref.shape[1]
        refs[-1][:, done : done + width] = part_ref[...]
        done += width


def beside(parts, after):
    shape = (parts[0].shape[0], sum(part.shape[1] for part in parts))
    return step(beside_kernel, parts, [(shape, parts[0].dtype)], after)[0]


def halve_kernel(keep_ref, came_ref, near_ref, send_ref):
    half = near_ref.shape[0]
    near_ref[...] = keep_ref[:half] + came_ref[:half].astype(jnp.float32)
    send_ref[...] = (keep_ref[half:] + came_ref[half:].astype(jnp.float32)).astype(jnp.bfloat16)


def halved(keep, came, after):
    half = (keep.shape[0] // 2, keep.shape[1])
    return step(halve_kernel, [keep, came], [(half, jnp.float32), (half, jnp.bfloat16)], after)


def lessen_kernel(keep_ref, came_ref, target_ref, sum_ref, send_ref):
    block = target_ref.shape[0]
    total = keep_ref[...] + came_ref[...].astype(jnp.float32)
    own = total[:block] - target_ref[...].astype(jnp.float32)
    sum_ref[:block] = own
    sum_ref[block:] = total[block:]
    send_ref[:block] = own.astype(jnp.bfloat16)
    send_ref[block:] = total[block:].astype(jnp.bfloat16)


def lessened(keep, came, target, after):
    both = [(keep.shape, jnp.float32), (keep.shape, jnp.bfloat16)]
    return step(lessen_kernel, [keep, came, target], both, after)


def close_kernel(keep_ref, came_ref, out_ref):
    block = keep_ref.shape[0] // 2
    near, far = came_ref[block:], came_ref[:block]
    out_ref[:block] = (keep_ref[:block] + near.astype(jnp.float32)).astype(jnp.bfloat16)
    out_ref[block:] = (keep_ref[block:] + far.astype(jnp.float32)).astype(jnp.bfloat16)


def closed(keep, came, after):
    return step(close_kernel, [keep, came], [(keep.shape, jnp.bfloat16)], after)[0]


def stack_kernel(own_ref, came_ref, out_ref):
    rows = own_ref.shape[0]
    out_ref[:rows] = own_ref[...]
    out_ref[rows:] = came_ref[...]


def stacked(own, came, after):
    shape = (2 * own.shape[0], own.shape[1])
    return step(stack_kernel, [own, came], [(shape, own.dtype)], after)[0]


def expanded(first_beam, weight, shift_x, shift_y, cutoff, imaginary, tile_count):
    local = weight.shape[1]
    half = SIDE // 2
    beam = first_beam + jnp.arange(local, dtype=jnp.int32)
    freq_x = (beam % SIDE - half)[:, None]
    freq_y = (beam // SIDE - half)[:, None]
    ramp = (freq_x * shift_x[None, :] + freq_y * shift_y[None, :]) % GRID
    phase = ramp.astype(jnp.float32) * (TWO_PI / GRID)
    inside = freq_x * freq_x + freq_y * freq_y <= cutoff[None, :]
    cosine = jnp.cos(phase)
    sine = jnp.sin(phase)
    w_real = weight[0][:, None]
    w_imag = weight[1][:, None]
    c_real = jnp.where(inside, w_real * cosine + w_imag * sine, 0.0).astype(jnp.bfloat16)
    c_imag = jnp.where(inside, w_imag * cosine - w_real * sine, 0.0).astype(jnp.bfloat16)
    by_real = jnp.where(imaginary, c_imag, c_real)
    by_imag = jnp.where(imaginary, c_real, -c_imag)
    step = GRID // TILE_SIDE
    window = shift_x // step * TILE_SIDE + shift_y // step
    onehot = window[None, :] == jnp.arange(tile_count, dtype=jnp.int32)[:, None]
    both = jnp.stack([by_real, by_imag])
    spread = jnp.where(onehot[None, None], both[:, :, None, :], jnp.zeros((), jnp.bfloat16))
    return spread.reshape(2 * local * tile_count, shift_x.shape[0])


def body(count, s_matrix, beam_weight, probe_shift, probe_cutoff, target, target_exp):
    _, local, tile_count, pixels = s_matrix.shape
    stages = count.bit_length() - 2
    own_probes = probe_cutoff.shape[0]
    block = 2 * own_probes
    params = jnp.concatenate([probe_shift.T, probe_cutoff[None]], axis=0)
    params = jnp.concatenate([params, params], axis=1)
    s_flat = s_matrix.reshape(2 * local * tile_count, pixels)
    depth = s_flat.shape[0] // PIECES
    width = pixels // CHUNKS
    pieces = [staged(s_flat, piece * depth, depth, width) for piece in range(PIECES)]
    params = gathered(params, count, pieces[:1])
    rows = params.shape[1]
    imaginary = (jnp.arange(rows, dtype=jnp.int32) // own_probes % 2 == 1)[None, :]
    at = expanded(
        lax.axis_index("beam") * local, beam_weight, params[0], params[1], params[2], imaginary, tile_count
    )
    scale = jnp.exp2(target_exp.astype(jnp.float32))[None, :, None]
    scaled = (target.astype(jnp.float32) * scale).astype(jnp.bfloat16).reshape(block, pixels)
    scaled = lax.optimization_barrier([scaled[:, c * width : (c + 1) * width] for c in range(CHUNKS)])
    states, after, total = [], [], s_flat.shape[0]
    for chunk in range(CHUNKS):
        columns = slice((chunk + 1) * width, (chunk + 2) * width)
        fetch = [(slice(row, row + total // 2), columns) for row in (0, total // 2)]
        fetch = fetch if chunk < CHUNKS - 1 else [None, None]
        send, *one = forward(at, pieces, rows // 2, jnp.bfloat16, s_flat, fetch[0], after)
        keep, *two = forward(at, pieces, 0, jnp.float32, s_flat, fetch[1], [send])
        pieces = one + two
        states.append(halved(keep, swap(send, count, -1), []))
        after = [states[-1][1]]
    for stage in range(stages - 1):
        for chunk in range(CHUNKS):
            keep, send = states[chunk]
            after = [states[chunk + 1][1]] if stage == 0 and chunk < CHUNKS - 1 else []
            came = swap(send, count, stage)
            if stage < stages - 2:
                states[chunk] = halved(keep, came, after)
            else:
                states[chunk] = lessened(keep, came, scaled[chunk], after)
    held = [closed(keep, swap(send, count, stages - 1), []) for keep, send in states]
    for stage in range(stages - 2, -1, -1):
        held = [stacked(part, swap(part, count, stage), []) for part in held]
    grad = None
    for chunk in range(CHUNKS):
        grad = backward(at, held[chunk], swap(held[chunk], count, -1), grad, chunk, pixels)
    return grad.reshape(2, local, tile_count, pixels)


def solution(mesh):
    return jax.shard_map(
        functools.partial(body, mesh.shape["beam"]),
        mesh=mesh,
        in_specs=(
            P(None, ("grp", "beam"), None, None),
            P(None, ("grp", "beam")),
            P(("grp", "beam"), None),
            P(("grp", "beam")),
            P(None, ("grp", "beam"), None),
            P(("grp", "beam")),
        ),
        out_specs=P(None, ("grp", "beam"), None, None),
        check_vma=False,
    )
```
